32 devices in a mesh: groups: 2 (over y), edge: 4 (over z), replica: 2 (over x), probe: 2 (over core).
Axes of the slice: x: 2, y: 2, z: 4, core: 2. Of those that a mesh axis runs over, the one named last changes fastest.
Arguments:
- edge_feats: bfloat16 [4, 6144, 256], P(('groups', 'replica'), 'edge'), parts along dimension 0, may hold values from -6 to 6
- edge_vecs: float32 [4, 3, 6144], P(('groups', 'replica'), None, 'edge'), parts along dimension 0, may hold values from -2 to 2
- senders: int32 [4, 6144], P(('groups', 'replica'), 'edge'), parts along dimension 0, may hold values from 0 to 1023
- receivers: int32 [4, 6144], P(('groups', 'replica'), 'edge'), parts along dimension 0, may hold values from 0 to 1023
- tiles: bfloat16 [4, 128, 128, 128], P(('groups', 'replica'), 'edge'), parts along dimension 0, may hold values from -0.5 to 0.5
- tile_rows: int32 [4, 128], P(('groups', 'replica'), 'edge'), parts along dimension 0, may hold values from 0 to 23
- tile_cols: int32 [4, 128], P(('groups', 'replica'), 'edge'), parts along dimension 0, may hold values from 0 to 23
- tile_count: int32 [4, 4], P(('groups', 'replica'), 'edge'), parts along dimension 0, may hold values from 1 to 32, as said below
- probes: int32 [3072, 128], P(None, 'probe'), may hold values from -1 to 1, as said below
- w_in: bfloat16 [256, 256], replicated, may hold values from -0.375 to 0.375
- w_msg: bfloat16 [256, 128], replicated, may hold values from -0.375 to 0.375
- w_stiff: bfloat16 [256], replicated, may hold values from -0.375 to 0.375
- w_env: float32 [128], replicated, may hold values from -0.1875 to 0.1875
Outputs:
- residual: float32 [4, 3072, 128], P(('groups', 'replica'), None, 'probe'), parts along dimension 0
- mse: float32 [4], P(('groups', 'replica')), parts along dimension 0
- grad_in: float32 [512, 256], P('groups'), parts along dimension 0
- grad_msg: float32 [512, 128], P('groups'), parts along dimension 0
- grad_stiff: float32 [512], P('groups'), parts along dimension 0
- grad_env: float32 [256], P('groups'), parts along dimension 0
The draws below stay inside these ranges and needn't reach their ends.
There are 2 independent parts, one for each index of `groups`. The reference program is written for one: setup_inputs(seed, part) draws one part's arguments, and reference() takes and returns one part's arrays. A program takes and returns all parts, laid end to end along the dimension named above; an argument that names none is the same for every part. Nothing has to cross between parts.
Inputs may be any that keep to these rules, and one draw needn't show every extreme that they name: `probes`: entries are -1 or 1. `tile_count`: in every structure some owner has all 32 slots live.
All inputs are finite; a program needn't handle non-finite values.
Results may differ from the reference program's by a relative error of at most 0.0018.
Values sent between devices are 32-bit elements; how exact they have to be, the bound alone decides.
A program may use at most 64 MiB of HBM per device.

```python
import jax
import jax.numpy as jnp
from jax import lax

LATENT = 256
MSG = 128
ATOMS = 1024
SLOTS = 32
TILE = 128
PROBES = 128
STRUCTS = 2
EDGES = 6144
TILE_SLOTS = 128
BLOCKS = 24
N_EDGE = 4


def draw_tile_count(key, part):
    key = jax.random.fold_in(key, 2)
    first, second = jax.random.split(key)
    counts = jax.random.randint(first, (STRUCTS, N_EDGE), 1, SLOTS // 2 + 1)
    fullest = jax.random.randint(second, (STRUCTS, 1), 0, N_EDGE)
    owners = jnp.arange(N_EDGE, dtype=jnp.int32)[None, :]
    return jnp.where(owners == fullest, SLOTS, counts).astype(jnp.int32)


def draw_probes(key, part):
    key = jax.random.fold_in(key, 1)
    return (jax.random.randint(key, (3 * ATOMS, PROBES), 0, 2) * 2 - 1).astype(jnp.int32)


def touch_ends(values, key, smallest, top_value):
    spot = [jax.random.randint(jax.random.fold_in(key, axis), (), 0, length) for axis, length in enumerate(values.shape)]
    widest = values.shape.index(max(values.shape))
    neighbour = spot[:widest] + [(spot[widest] + 1) % values.shape[widest]] + spot[widest + 1:]
    return values.at[tuple(spot)].set(smallest).at[tuple(neighbour)].set(top_value)


def block_scale(rng, shape, pieces, low, largest):
    gain = 1.0
    for dim, parts in pieces:
        heights = jax.random.uniform(jax.random.fold_in(jax.random.fold_in(rng, 6), dim), (parts,), jnp.float32, low / len(pieces), largest / len(pieces))
        gain = gain * jnp.repeat(jnp.exp(heights), shape[dim] // parts).reshape((-1,) + (1,) * (len(shape) - 1 - dim))
    return gain


def bell_draw(key, extent, width, reach, cuts=(), held_as=jnp.bfloat16):
    entries = jax.random.normal(key, extent, jnp.float32) * width
    if len(cuts) > 0:
        entries = block_scale(key, extent, cuts, -0.22, 0.18) * entries
    return jnp.clip(entries, min=-reach, max=reach).astype(held_as)


def setup_inputs(seed: int = 0, part: int = 0) -> dict:
    key_list = jax.random.split(jax.random.key(seed), 14)
    part_splits = jax.random.split(jax.random.fold_in(key_list[13], part), 14)
    edge_feats = bell_draw(part_splits[0], (STRUCTS, EDGES, LATENT), 1.0, 6.0, ((0, 2), (1, 4)))
    edge_vecs = bell_draw(part_splits[1], (STRUCTS, 3, EDGES), 0.3, 2.0, ((0, 2), (2, 4)), jnp.float32)
    senders = touch_ends(jax.random.randint(part_splits[2], (STRUCTS, EDGES), 0, ATOMS), jax.random.fold_in(part_splits[2], 1), 0, ATOMS - 1).astype(jnp.int32)
    receivers = touch_ends(jax.random.randint(part_splits[3], (STRUCTS, EDGES), 0, ATOMS), jax.random.fold_in(part_splits[3], 1), 0, ATOMS - 1).astype(jnp.int32)
    tiles = bell_draw(part_splits[4], (STRUCTS, TILE_SLOTS, TILE, TILE), TILE ** -0.5, 0.5, ((0, 2), (1, 4)))
    tile_rows = touch_ends(jax.random.randint(part_splits[5], (STRUCTS, TILE_SLOTS), 0, BLOCKS), jax.random.fold_in(part_splits[5], 1), 0, BLOCKS - 1).astype(jnp.int32)
    tile_cols = touch_ends(jax.random.randint(part_splits[6], (STRUCTS, TILE_SLOTS), 0, BLOCKS), jax.random.fold_in(part_splits[6], 1), 0, BLOCKS - 1).astype(jnp.int32)
    tile_count = draw_tile_count(jax.random.fold_in(jax.random.fold_in(key_list[13], part), 71), part)
    probes = draw_probes(jax.random.fold_in(key_list[13], 71), part)
    w_in = bell_draw(key_list[9], (LATENT, LATENT), LATENT ** -0.5, 0.375)
    w_msg = bell_draw(key_list[10], (LATENT, MSG), LATENT ** -0.5, 0.375)
    w_stiff = bell_draw(key_list[11], (LATENT,), LATENT ** -0.5, 0.375)
    w_env = bell_draw(key_list[12], (MSG,), (8 * MSG) ** -0.5, 0.1875, (), jnp.float32)
    return {"edge_feats": edge_feats, "edge_vecs": edge_vecs, "senders": senders, "receivers": receivers, "tiles": tiles, "tile_rows": tile_rows, "tile_cols": tile_cols, "tile_count": tile_count, "probes": probes, "w_in": w_in, "w_msg": w_msg, "w_stiff": w_stiff, "w_env": w_env}


HI = lax.Precision.HIGHEST


def one_structure(feats, vecs, send, recv, tls, rows, cols, count, probes, w_in, w_msg, w_stiff, w_env):
    pre = jnp.dot(feats, w_in, preferred_element_type=jnp.float32)
    latent = jax.nn.silu(pre).astype(jnp.bfloat16)
    message = jnp.dot(latent, w_msg, preferred_element_type=jnp.float32).astype(jnp.bfloat16)
    env = jax.ops.segment_sum(message.astype(jnp.float32), recv, ATOMS)
    env_recv = env[recv]
    zeta = jnp.dot(latent, w_stiff, preferred_element_type=jnp.float32) + jnp.dot(env_recv, w_env, precision=HI)
    stiff = jax.nn.softplus(zeta)
    pmat = probes.astype(jnp.float32).reshape(ATOMS, 3, PROBES)
    delta = pmat[send] - pmat[recv]
    proj = jnp.einsum('ce,ecp->ep', vecs, delta, precision=HI)
    contrib = (stiff[:, None, None] * vecs.T[:, :, None] * proj[:, None, :]).astype(jnp.bfloat16)
    contrib = contrib.astype(jnp.float32)
    model_hvp = jax.ops.segment_sum(contrib, send, ATOMS) - jax.ops.segment_sum(contrib, recv, ATOMS)
    model_hvp = model_hvp.reshape(3 * ATOMS, PROBES)
    slot = jnp.arange(TILE_SLOTS, dtype=jnp.int32)
    live = (slot % SLOTS < count[slot // SLOTS]).astype(jnp.float32)
    blocks = probes.astype(jnp.float32).reshape(BLOCKS, TILE, PROBES)[cols]
    prod = jnp.einsum('tij,tjp->tip', tls.astype(jnp.float32), blocks, precision=HI) * live[:, None, None]
    ref_hvp = jax.ops.segment_sum(prod, rows, BLOCKS).reshape(3 * ATOMS, PROBES)
    residual = model_hvp - ref_hvp
    mse = jnp.sum(residual * residual) / (3 * ATOMS * PROBES)
    rres = residual.reshape(ATOMS, 3, PROBES)
    rdiff = rres[send] - rres[recv]
    rproj = jnp.einsum('ce,ecp->ep', vecs, rdiff, precision=HI)
    dstiff = (2.0 / PROBES) * jnp.sum(proj * rproj, axis=1)
    dzeta = dstiff * jax.nn.sigmoid(zeta)
    dzeta_b = dzeta.astype(jnp.bfloat16)
    weight = jax.ops.segment_sum(dzeta, recv, ATOMS)
    dmsg = (weight[recv][:, None] * w_env[None, :]).astype(jnp.bfloat16)
    dlat = dzeta[:, None] * w_stiff.astype(jnp.float32)[None, :] + jnp.dot(dmsg, w_msg.T, preferred_element_type=jnp.float32)
    sig = jax.nn.sigmoid(pre)
    dpre = (dlat * sig * (1.0 + pre * (1.0 - sig))).astype(jnp.bfloat16)
    g_in = jnp.dot(feats.T, dpre, preferred_element_type=jnp.float32)
    g_msg = jnp.dot(latent.T, dmsg, preferred_element_type=jnp.float32)
    g_stiff = jnp.dot(dzeta_b, latent, preferred_element_type=jnp.float32)
    g_env = jnp.dot(dzeta, env_recv, precision=HI)
    return residual, mse, g_in, g_msg, g_stiff, g_env


def reference(edge_feats, edge_vecs, senders, receivers, tiles, tile_rows, tile_cols, tile_count, probes, w_in, w_msg, w_stiff, w_env):
    residuals = []
    errors = []
    totals = None
    for index in range(STRUCTS):
        result = one_structure(edge_feats[index], edge_vecs[index], senders[index], receivers[index], tiles[index], tile_rows[index], tile_cols[index], tile_count[index], probes, w_in, w_msg, w_stiff, w_env)
        residuals.append(result[0])
        errors.append(result[1])
        grads = result[2:]
        totals = grads if totals is None else tuple(a + b for a, b in zip(totals, grads))
    return jnp.stack(residuals), jnp.stack(errors), totals[0], totals[1], totals[2], totals[3]
```

```python
import functools

import jax
import jax.numpy as jnp
from jax import lax
from jax.experimental import pallas as pl
from jax.experimental.pallas import tpu as pltpu
from jax.sharding import PartitionSpec as P

TILE = 128
MESH = pl.DeviceIdType.MESH
F32 = jnp.float32
BF16 = jnp.bfloat16
NN = (((1,), (0,)), ((), ()))
NT = (((1,), (1,)), ((), ()))
TN = (((0,), (0,)), ((), ()))


def dot(a, b, dims=NN):
    return lax.dot_general(a, b, dims, preferred_element_type=F32)


def split(x, parts):
    out = []
    for _ in range(parts):
        piece = x.astype(BF16)
        out.append(piece)
        x = x - piece.astype(F32)
    return out


def stack_rows(rows):
    n = rows[0].shape[1]
    where = lax.broadcasted_iota(jnp.int32, (8, n), 0)
    out = jnp.zeros((8, n), F32)
    for i, row in enumerate(rows):
        out = jnp.where(where == i, row.astype(F32), out)
    return out.astype(BF16)


def row_dot(x, b, dims=NN, parts=3):
    return jnp.sum(dot(stack_rows(split(x, parts)), b, dims), axis=0, keepdims=True)


def sigmoid(x):
    return 1.0 / (1.0 + jnp.exp(-x))


def loop(count, fn):
    if count <= 16:
        for i in range(count):
            fn(i)
    else:
        def step(i, carry):
            fn(i)
            return carry
        lax.fori_loop(0, count, step, 0)


def tile_kernel(rows, cols, count, tiles, probes, pt_ref, ref_ref, pb, pf, acc):
    n_slots = tiles.shape[1]
    atoms = pt_ref.shape[1]
    share = probes.shape[1]
    pv = probes[...].astype(F32)
    pf[:, :share] = pv
    pb[...] = pv.astype(BF16).reshape(pb.shape)
    acc[...] = jnp.zeros_like(acc)
    live = count[0, 0]
    unroll = 8 if n_slots % 8 == 0 else 1

    def step(i, carry):
        for j in range(unroll):
            t = i * unroll + j
            prod = dot(tiles[0, t], pb[cols[0, t]])
            prod = jnp.where(t < live, prod, 0.0)
            at = pl.ds(pl.multiple_of(rows[0, t] * TILE, TILE), TILE)
            acc[at, :share] += prod
        return carry

    lax.fori_loop(0, (live + unroll - 1) // unroll, step, 0)
    for c in range(3):
        pick = pl.ds(c, atoms, stride=3)
        pt_ref[c * share:(c + 1) * share, :] = pf[pick, :].T[:share].astype(BF16)
        ref_ref[c * share:(c + 1) * share, :] = acc[pick, :].T[:share]


def main_kernel(
    n_e, n_r, n_p, probes_total,
    feats, vecs, send, recv, pt, refs, w_in, w_msg, w_stiff, w_env,
    res_out, mse_out, gin_out, gmsg_out, gstiff_out, genv_out,
    hot_r, hot_s, pre, latent, proj, contrib, rd,
    s_buf, part_buf, got_buf, r_buf, w_buf, z_buf, g_buf, gg_buf, gf_buf, v_buf,
    s_ss, s_rs, rs_ss, rs_rs, ag_ss, ag_rs, w_ss, w_rs, z_ss, z_rs, g_ss, g_rs, gf_ss, gf_rs, v_ss, v_rs,
):
    edges = send.shape[1]
    atoms = pt.shape[1]
    share = pt.shape[0] // 3
    width = w_in.shape[1]
    half = width // n_p
    own_n, piece = r_buf.shape[0], r_buf.shape[2]
    lanes = 256
    me_e, me_r, me_p = lax.axis_index("edge"), lax.axis_index("replica"), lax.axis_index("probe")

    def dev(e, r, p):
        return {"edge": e, "replica": r, "probe": p}

    def copy(src, dst, ss, rs, device):
        return pltpu.make_async_remote_copy(
            src_ref=src, dst_ref=dst, send_sem=ss, recv_sem=rs, device_id=device, device_id_type=MESH)

    barrier = pltpu.get_barrier_semaphore()
    n_all = n_e * n_r * n_p
    me_all = (me_e * n_r + me_r) * n_p + me_p

    def all_dev(f):
        return dev(f // (n_r * n_p), (f // n_p) % n_r, f % n_p)

    def greet(i):
        pl.semaphore_signal(barrier, inc=1, device_id=all_dev((me_all + i + 1) % n_all), device_id_type=MESH)

    loop(n_all - 1, greet)

    def spread(buf, ss, rs, me, n, device):
        def go(i):
            copy(buf.at[me], buf.at[me], ss.at[i], rs.at[me], device((me + i + 1) % n)).start()
        loop(n - 1, go)

    def gathered(buf, ss, rs, me, n, device):
        def go(i):
            j = (me + i + 1) % n
            c = copy(buf.at[j], buf.at[j], ss.at[i], rs.at[j], device(j))
            c.wait_recv()
            c.wait_send()
        loop(n - 1, go)

    def total(buf, n):
        if n <= 16:
            out = buf[0]
            for j in range(1, n):
                out = out + buf[j]
            return out
        return lax.fori_loop(1, n, lambda j, t: t + buf[j], buf[0])

    wenv = w_env[...]
    u = row_dot(wenv, w_msg[...], NT)
    u_hi, u_lo = split(u, 2)
    readout = stack_rows([w_stiff[...], u_hi, u_lo])
    rows = 256 if edges % 256 == 0 else edges

    def forward(i, carry):
        at = pl.ds(pl.multiple_of(i * rows, rows), rows)
        x = dot(feats[0, at, :], w_in[...])
        for p in range(n_p):
            pre[p, at, :] = x[:, p * half:(p + 1) * half]
        latent[at, :] = (x * sigmoid(x)).astype(BF16)
        return carry

    lax.fori_loop(0, edges // rows, forward, 0)

    snd, rcv = send[...], recv[...]

    def hots(i, carry):
        base = i * 32
        ids = lax.broadcasted_iota(jnp.int32, (32, edges), 0) + base
        at = pl.ds(pl.multiple_of(base, 32), 32)
        r = jnp.where(ids == rcv, 1.0, 0.0)
        s = jnp.where(ids == snd, 1.0, 0.0)
        hot_r[at, :] = r.astype(BF16)
        hot_s[at, :] = (s - r).astype(BF16)
        return carry

    lax.fori_loop(0, atoms // 32, hots, 0)
    read = dot(readout, latent[...], NT)
    lw = read[0:1]
    mw = read[1:2] + read[2:3]
    s_buf[me_e] = row_dot(mw, hot_r[...], NT)
    pl.semaphore_wait(barrier, n_all - 1)
    edge_dev = lambda e: dev(e, me_r, me_p)
    spread(s_buf, s_ss, s_rs, me_e, n_e, edge_dev)

    vec = [vecs[0, c:c + 1, :] for c in range(3)]

    def project(i, carry):
        at = pl.ds(pl.multiple_of(i * lanes, lanes), lanes)
        delta = dot(pt[...], hot_s[:, at])
        v = vecs[0, :, at]
        out = v[0:1] * delta[:share]
        for c in (1, 2):
            out = out + v[c:c + 1] * delta[c * share:(c + 1) * share]
        proj[:, at] = out
        return carry

    lax.fori_loop(0, edges // lanes, project, 0)
    gathered(s_buf, s_ss, s_rs, me_e, n_e, edge_dev)
    zeta = lw + row_dot(total(s_buf, n_e), hot_r[...])
    stiff = jnp.maximum(zeta, 0.0) + jnp.log1p(jnp.exp(-jnp.abs(zeta)))
    sig_z = sigmoid(zeta)
    for c in range(3):
        contrib[c * share:(c + 1) * share, :] = (stiff * vec[c] * proj[...]).astype(BF16)

    def model(q):
        at = pl.ds(pl.multiple_of(q * piece, piece), piece)
        return dot(contrib[...], hot_s[at, :], NT) - refs[:, at]

    def rs_copy(i, q, src):
        return copy(part_buf.at[q], got_buf.at[src], rs_ss.at[i], rs_rs.at[src], edge_dev(q))

    def send_piece(i):
        q = (me_e + i + 1) % n_e

        def go():
            part_buf[q] = model(q)
            rs_copy(i, q, me_e).start()

        if own_n == n_e:
            go()
        else:
            pl.when(q < own_n)(go)

    loop(n_e - 1, send_piece)

    def own():
        got_buf[me_e] = model(me_e)

        def wait(i):
            j = (me_e + i + 1) % n_e
            copy(got_buf.at[j], got_buf.at[j], rs_ss.at[i], rs_rs.at[j], edge_dev(j)).wait_recv()

        loop(n_e - 1, wait)
        r_buf[me_e] = total(got_buf, n_e)

        def give(i):
            q = (me_e + i + 1) % n_e
            copy(r_buf.at[me_e], r_buf.at[me_e], ag_ss.at[i], ag_rs.at[me_e], edge_dev(q)).start()

        loop(n_e - 1, give)

    if own_n == n_e:
        own()
    else:
        pl.when(me_e < own_n)(own)

    rd[...] = jnp.zeros_like(rd)

    def use(q, square):
        r = r_buf[q]
        hi, lo = split(r, 2)
        both = jnp.concatenate([hi, lo], axis=0)
        at = pl.ds(pl.multiple_of(q * piece, piece), piece)
        for i in range(edges // lanes):
            cut = slice(i * lanes, (i + 1) * lanes)
            x = dot(both, hot_s[at, cut])
            rd[:, cut] += x[:3 * share] + x[3 * share:]
        return square + jnp.sum(jnp.sum(r * r, axis=0, keepdims=True), axis=1, keepdims=True)

    square = jnp.zeros((1, 1), F32)
    for i in range(n_e):
        q = (me_e + i) % n_e
        if i:
            def wait(q=q):
                copy(r_buf.at[q], r_buf.at[q], ag_ss.at[0], ag_rs.at[q], edge_dev(q)).wait_recv()
            if own_n == n_e:
                wait()
            else:
                pl.when(q < own_n)(wait)
        if own_n == n_e:
            square = use(q, square)
    if own_n != n_e:
        square = lax.fori_loop(0, own_n, use, square)

    rproj = vec[0] * rd[:share]
    for c in (1, 2):
        rproj = rproj + vec[c] * rd[c * share:(c + 1) * share]
    dst = (2.0 / probes_total) * jnp.sum(proj[...] * rproj, axis=0, keepdims=True)
    dz_part = dst * sig_z
    n_w = n_e * n_p
    me_w = me_e * n_p + me_p
    w_dev = lambda f: dev(f // n_p, me_r, f % n_p)
    p_dev = lambda p: dev(me_e, me_r, p)
    w_buf[me_w, :, :atoms] = row_dot(dz_part, hot_r[...], NT)
    w_buf[me_w, :, atoms:] = jnp.broadcast_to(square, (1, 128))
    z_buf[me_p] = dz_part
    spread(w_buf, w_ss, w_rs, me_w, n_w, w_dev)
    spread(z_buf, z_ss, z_rs, me_p, n_p, p_dev)

    for q in range(own_n):
        for c in range(3):
            x = r_buf[q, c * share:(c + 1) * share, :]
            res_out[pl.ds(q * piece * 3 + c, piece, stride=3), :] = x.T

    gathered(w_buf, w_ss, w_rs, me_w, n_w, w_dev)
    gathered(z_buf, z_ss, z_rs, me_p, n_p, p_dev)
    weight = total(w_buf, n_w)[:, :atoms]
    squares = w_buf[me_e * n_p, :, atoms:]
    for p in range(1, n_p):
        squares = squares + w_buf[me_e * n_p + p, :, atoms:]
    mse_out[...] = squares / (3 * atoms * probes_total)
    dz = total(z_buf, n_p)
    wr = row_dot(weight, hot_r[...])

    dz_hi, dz_lo = split(dz, 2)
    wr_hi, wr_lo = split(wr, 2)
    sums = dot(stack_rows([dz_hi, dz_lo, wr_hi, wr_lo]), latent[...])
    g_members = n_e * n_r
    me_g = me_e * n_r + me_r
    g_dev = lambda f: dev(f // n_r, f % n_r, me_p)
    v_buf[me_g] = jnp.zeros(v_buf.shape[1:], F32)
    v_buf[me_g, 0:1] = sums[0:1] + sums[1:2]
    v_buf[me_g, 1:2] = sums[2:3] + sums[3:4]
    spread(v_buf, v_ss, v_rs, me_g, g_members, g_dev)

    ws = w_stiff[...].astype(F32)
    ws_half = ws[:, :half]
    u_half = u[:, :half]
    for p in range(1, n_p):
        ws_half = jnp.where(me_p == p, ws[:, p * half:(p + 1) * half], ws_half)
        u_half = jnp.where(me_p == p, u[:, p * half:(p + 1) * half], u_half)
    uh_hi, uh_lo = split(u_half, 2)
    dlat = dot(
        stack_rows([dz_hi, dz_lo, wr_hi, wr_hi, wr_lo]),
        stack_rows([ws_half, ws_half, uh_hi, uh_lo, uh_hi]), TN)
    x = pre[me_p]
    sg = sigmoid(x)
    dpre = (dlat * sg * (1.0 + x * (1.0 - sg))).astype(BF16)
    g_half = dot(feats[0], dpre, TN)
    g_own, g_rows = gf_buf.shape[1], gf_buf.shape[2]
    g_buf[...] = g_half.reshape(g_buf.shape)

    def g_send(i):
        q = (me_g + i + 1) % g_members

        def go():
            copy(g_buf.at[q], gg_buf.at[me_g], g_ss.at[i], g_rs.at[me_g], g_dev(q)).start()

        if g_own == g_members:
            go()
        else:
            pl.when(q < g_own)(go)

    loop(g_members - 1, g_send)

    def gf_copy(i, g, p, f):
        return copy(gf_buf.at[p, g], gf_buf.at[p, g], gf_ss.at[i], gf_rs.at[p, g], all_dev(f))

    def g_own_part():
        gg_buf[me_g] = g_buf[me_g]

        def wait(i):
            j = (me_g + i + 1) % g_members
            copy(gg_buf.at[j], gg_buf.at[j], g_ss.at[i], g_rs.at[j], g_dev(j)).wait_recv()

        loop(g_members - 1, wait)
        gf_buf[me_p, me_g] = total(gg_buf, g_members)

        def give(i):
            gf_copy(i, me_g, me_p, (me_all + i + 1) % n_all).start()

        loop(n_all - 1, give)

    if g_own == g_members:
        g_own_part()
    else:
        pl.when(me_g < g_own)(g_own_part)

    gathered(v_buf, v_ss, v_rs, me_g, g_members, g_dev)
    v = total(v_buf, g_members)
    gstiff_out[...] = v[0:1]
    q_row = v[1:2]
    q_hi, q_lo = split(q_row, 2)
    e_hi, e_lo = split(wenv, 2)
    gmsg_out[...] = dot(stack_rows([q_hi, q_hi, q_lo]), stack_rows([e_hi, e_lo, e_hi]), TN)
    genv_out[...] = row_dot(q_row, w_msg[...])

    def g_arrive(i):
        f = (me_all + i + 1) % n_all
        p, g = f % n_p, f // n_p

        def go():
            gf_copy(i, g, p, f).wait_recv()

        if g_own == g_members:
            go()
        else:
            pl.when(g < g_own)(go)

    loop(n_all - 1, g_arrive)
    for p in range(n_p):
        gin_out[:, p * half:(p + 1) * half] = gf_buf[p].reshape(width, half)

    def sent(i):
        q = (me_e + i + 1) % n_e

        def go():
            rs_copy(i, q, me_e).wait_send()

        if own_n == n_e:
            go()
        else:
            pl.when(q < own_n)(go)

    loop(n_e - 1, sent)

    def ag_sent():
        loop(n_e - 1, lambda i: copy(
            r_buf.at[me_e], r_buf.at[me_e], ag_ss.at[i], ag_rs.at[me_e], edge_dev((me_e + i + 1) % n_e)).wait_send())

    if own_n == n_e:
        ag_sent()
    else:
        pl.when(me_e < own_n)(ag_sent)

    def g_sent(i):
        q = (me_g + i + 1) % g_members

        def go():
            copy(g_buf.at[q], gg_buf.at[me_g], g_ss.at[i], g_rs.at[me_g], g_dev(q)).wait_send()

        if g_own == g_members:
            go()
        else:
            pl.when(q < g_own)(go)

    loop(g_members - 1, g_sent)

    def gf_sent():
        loop(n_all - 1, lambda i: gf_copy(i, me_g, me_p, (me_all + i + 1) % n_all).wait_send())

    if g_own == g_members:
        gf_sent()
    else:
        pl.when(me_g < g_own)(gf_sent)


def body(
    n_e, n_r, n_p,
    edge_feats, edge_vecs, senders, receivers, tiles, tile_rows, tile_cols, tile_count,
    probes, w_in, w_msg, w_stiff, w_env,
):
    share = probes.shape[1]
    dim = probes.shape[0]
    atoms = dim // 3
    edges = senders.shape[1]
    width = w_in.shape[1]
    msg = w_msg.shape[1]
    vm = pl.BlockSpec(memory_space=pltpu.VMEM)
    sm = pl.BlockSpec(memory_space=pltpu.SMEM)
    pt, refs = pl.pallas_call(
        tile_kernel,
        out_shape=(
            jax.ShapeDtypeStruct((3 * share, atoms), BF16),
            jax.ShapeDtypeStruct((3 * share, atoms), F32),
        ),
        in_specs=[sm, sm, sm, vm, vm],
        out_specs=(vm, vm),
        scratch_shapes=[
            pltpu.VMEM((dim // TILE, TILE, share), BF16),
            pltpu.VMEM((dim, 128), F32),
            pltpu.VMEM((dim, 128), F32),
        ],
        compiler_params=pltpu.CompilerParams(vmem_limit_bytes=40 * 2**20),
        name="tiles",
    )(tile_rows, tile_cols, tile_count, tiles, probes)

    own_n = min(n_e, atoms // 128)
    piece = atoms // own_n
    g_members = n_e * n_r
    g_own = min(g_members, width // 8)
    g_rows = width // g_own
    half = width // n_p
    n_all = n_e * n_r * n_p
    n_w = n_e * n_p
    sem = lambda *shape: pltpu.SemaphoreType.DMA(shape)
    vmem = pltpu.VMEM
    outs = pl.pallas_call(
        functools.partial(main_kernel, n_e, n_r, n_p, share * n_p),
        out_shape=(
            jax.ShapeDtypeStruct((dim, share), F32),
            jax.ShapeDtypeStruct((1, 128), F32),
            jax.ShapeDtypeStruct((width, width), F32),
            jax.ShapeDtypeStruct((width, msg), F32),
            jax.ShapeDtypeStruct((1, width), F32),
            jax.ShapeDtypeStruct((1, msg), F32),
        ),
        in_specs=[vm] * 10,
        out_specs=(vm,) * 6,
        scratch_shapes=[
            vmem((atoms, edges), BF16),
            vmem((atoms, edges), BF16),
            vmem((n_p, edges, half), F32),
            vmem((edges, width), BF16),
            vmem((share, edges), F32),
            vmem((3 * share, edges), BF16),
            vmem((3 * share, edges), F32),
            vmem((n_e, 1, atoms), F32),
            vmem((own_n, 3 * share, piece), F32),
            vmem((n_e, 3 * share, piece), F32),
            vmem((own_n, 3 * share, piece), F32),
            vmem((n_w, 1, atoms + 128), F32),
            vmem((n_p, 1, edges), F32),
            vmem((g_own, g_rows, half), F32),
            vmem((g_members, g_rows, half), F32),
            vmem((n_p, g_own, g_rows, half), F32),
            vmem((g_members, 8, width), F32),
            sem(n_e), sem(n_e),
            sem(n_e), sem(n_e),
            sem(n_e), sem(n_e),
            sem(n_w), sem(n_w),
            sem(n_p), sem(n_p),
            sem(g_members), sem(g_members),
            sem(n_all), sem(n_p, g_members),
            sem(g_members), sem(g_members),
        ],
        compiler_params=pltpu.CompilerParams(
            collective_id=0, has_side_effects=True, vmem_limit_bytes=48 * 2**20),
        name="edges",
    )(
        edge_feats, edge_vecs, senders, receivers, pt, refs, w_in, w_msg,
        w_stiff.reshape(1, -1), w_env.reshape(1, -1),
    )
    residual, mse, g_in, g_msg, g_stiff, g_env = outs
    return (residual[None], mse[0, :1], g_in, g_msg, g_stiff[0], g_env[0])


def solution(mesh):
    n_e, n_r, n_p = mesh.shape["edge"], mesh.shape["replica"], mesh.shape["probe"]
    return jax.shard_map(
        functools.partial(body, n_e, n_r, n_p),
        mesh=mesh,
        in_specs=(
            P(("groups", "replica"), "edge", None),
            P(("groups", "replica"), None, "edge"),
            P(("groups", "replica"), "edge"),
            P(("groups", "replica"), "edge"),
            P(("groups", "replica"), "edge", None, None),
            P(("groups", "replica"), "edge"),
            P(("groups", "replica"), "edge"),
            P(("groups", "replica"), "edge"),
            P(None, "probe"),
            P(),
            P(),
            P(),
            P(),
        ),
        out_specs=(
            P(("groups", "replica"), None, "probe"),
            P(("groups", "replica")),
            P("groups", None),
            P("groups", None),
            P("groups"),
            P("groups"),
        ),
        check_vma=False,
    )
```

```python
import functools

import jax
import jax.numpy as jnp
from jax import lax
from jax.experimental import pallas as pl
from jax.experimental.pallas import tpu as pltpu
from jax.sharding import PartitionSpec as P

TILE = 128
MESH = pl.DeviceIdType.MESH
F32 = jnp.float32
BF16 = jnp.bfloat16
NN = (((1,), (0,)), ((), ()))
NT = (((1,), (1,)), ((), ()))
TN = (((0,), (0,)), ((), ()))


def dot(a, b, dims=NN):
    return lax.dot_general(a, b, dims, preferred_element_type=F32)


def split(x, parts):
    out = []
    for _ in range(parts):
        piece = x.astype(BF16)
        out.append(piece)
        x = x - piece.astype(F32)
    return out


def stack_rows(rows):
    n = rows[0].shape[1]
    where = lax.broadcasted_iota(jnp.int32, (8, n), 0)
    out = jnp.zeros((8, n), F32)
    for i, row in enumerate(rows):
        out = jnp.where(where == i, row.astype(F32), out)
    return out.astype(BF16)


def row_dot(x, b, dims=NN, parts=3):
    return jnp.sum(dot(stack_rows(split(x, parts)), b, dims), axis=0, keepdims=True)


def sigmoid(x):
    return 1.0 / (1.0 + jnp.exp(-x))


def loop(count, fn):
    if count <= 16:
        for i in range(count):
            fn(i)
    else:
        def step(i, carry):
            fn(i)
            return carry
        lax.fori_loop(0, count, step, 0)


def tile_kernel(rows, cols, count, tiles, probes, pt_ref, ref_ref, pb, pf, acc):
    n_slots = tiles.shape[1]
    atoms = pt_ref.shape[1]
    share = probes.shape[1]
    pv = probes[...].astype(F32)
    pf[:, :share] = pv
    pb[...] = pv.astype(BF16).reshape(pb.shape)
    acc[...] = jnp.zeros_like(acc)
    live = count[0, 0]
    unroll = 8 if n_slots % 8 == 0 else 1

    def step(i, carry):
        for j in range(unroll):
            t = i * unroll + j
            prod = dot(tiles[0, t], pb[cols[0, t]])
            prod = jnp.where(t < live, prod, 0.0)
            at = pl.ds(pl.multiple_of(rows[0, t] * TILE, TILE), TILE)
            acc[at, :share] += prod
        return carry

    lax.fori_loop(0, (live + unroll - 1) // unroll, step, 0)
    for c in range(3):
        pick = pl.ds(c, atoms, stride=3)
        pt_ref[c * share:(c + 1) * share, :] = pf[pick, :].T[:share].astype(BF16)
        ref_ref[c * share:(c + 1) * share, :] = acc[pick, :].T[:share]


def main_kernel(
    n_e, n_r, n_p, probes_total,
    feats, vecs, send, recv, pt, refs, w_in, w_msg, w_stiff, w_env,
    res_out, mse_out, gin_out, gmsg_out, gstiff_out, genv_out,
    hot_r, hot_s, pre, latent, proj, contrib, rd,
    s_buf, part_buf, got_buf, y_buf, r_buf, w_buf, z_buf, g_buf, gg_buf, gf_buf, v_buf,
    s_ss, s_rs, rs_ss, rs_rs, y_ss, y_rs, ag_ss, ag_rs, w_ss, w_rs, z_ss, z_rs, g_ss, g_rs, gf_ss, gf_rs, v_ss, v_rs,
):
    edges = send.shape[1]
    atoms = pt.shape[1]
    share = pt.shape[0] // 3
    width = w_in.shape[1]
    half = width // n_p
    own_n, piece = r_buf.shape[0], r_buf.shape[2]
    lanes = 256
    me_e, me_r, me_p = lax.axis_index("edge"), lax.axis_index("replica"), lax.axis_index("probe")

    def dev(e, r, p):
        return {"edge": e, "replica": r, "probe": p}

    def copy(src, dst, ss, rs, device):
        return pltpu.make_async_remote_copy(
            src_ref=src, dst_ref=dst, send_sem=ss, recv_sem=rs, device_id=device, device_id_type=MESH)

    barrier = pltpu.get_barrier_semaphore()
    n_all = n_e * n_r * n_p
    me_all = (me_e * n_r + me_r) * n_p + me_p

    def all_dev(f):
        return dev(f // (n_r * n_p), (f // n_p) % n_r, f % n_p)

    def greet(i):
        pl.semaphore_signal(barrier, inc=1, device_id=all_dev((me_all + i + 1) % n_all), device_id_type=MESH)

    loop(n_all - 1, greet)

    def spread(buf, ss, rs, me, n, device):
        def go(i):
            copy(buf.at[me], buf.at[me], ss.at[i], rs.at[me], device((me + i + 1) % n)).start()
        loop(n - 1, go)

    def gathered(buf, ss, rs, me, n, device):
        def go(i):
            j = (me + i + 1) % n
            c = copy(buf.at[j], buf.at[j], ss.at[i], rs.at[j], device(j))
            c.wait_recv()
            c.wait_send()
        loop(n - 1, go)

    def total(buf, n):
        if n <= 16:
            out = buf[0]
            for j in range(1, n):
                out = out + buf[j]
            return out
        return lax.fori_loop(1, n, lambda j, t: t + buf[j], buf[0])

    wenv = w_env[...]
    u = row_dot(wenv, w_msg[...], NT)
    u_hi, u_lo = split(u, 2)
    readout = stack_rows([w_stiff[...], u_hi, u_lo])
    rows = 256 if edges % 256 == 0 else edges

    def forward(i, carry):
        at = pl.ds(pl.multiple_of(i * rows, rows), rows)
        x = dot(feats[0, at, :], w_in[...])
        for p in range(n_p):
            pre[p, at, :] = x[:, p * half:(p + 1) * half]
        latent[at, :] = (x * sigmoid(x)).astype(BF16)
        return carry

    lax.fori_loop(0, edges // rows, forward, 0)

    snd, rcv = send[...], recv[...]

    def hots(i, carry):
        base = i * 32
        ids = lax.broadcasted_iota(jnp.int32, (32, edges), 0) + base
        at = pl.ds(pl.multiple_of(base, 32), 32)
        r = jnp.where(ids == rcv, 1.0, 0.0)
        s = jnp.where(ids == snd, 1.0, 0.0)
        hot_r[at, :] = r.astype(BF16)
        hot_s[at, :] = (s - r).astype(BF16)
        return carry

    lax.fori_loop(0, atoms // 32, hots, 0)
    read = dot(readout, latent[...], NT)
    lw = read[0:1]
    mw = read[1:2] + read[2:3]
    s_buf[me_e] = row_dot(mw, hot_r[...], NT)
    pl.semaphore_wait(barrier, n_all - 1)
    edge_dev = lambda e: dev(e, me_r, me_p)
    spread(s_buf, s_ss, s_rs, me_e, n_e, edge_dev)

    vec = [vecs[0, c:c + 1, :] for c in range(3)]

    def project(i, carry):
        at = pl.ds(pl.multiple_of(i * lanes, lanes), lanes)
        delta = dot(pt[...], hot_s[:, at])
        v = vecs[0, :, at]
        out = v[0:1] * delta[:share]
        for c in (1, 2):
            out = out + v[c:c + 1] * delta[c * share:(c + 1) * share]
        proj[:, at] = out
        return carry

    lax.fori_loop(0, edges // lanes, project, 0)
    gathered(s_buf, s_ss, s_rs, me_e, n_e, edge_dev)
    zeta = lw + row_dot(total(s_buf, n_e), hot_r[...])
    stiff = jnp.maximum(zeta, 0.0) + jnp.log1p(jnp.exp(-jnp.abs(zeta)))
    sig_z = sigmoid(zeta)
    for c in range(3):
        contrib[c * share:(c + 1) * share, :] = (stiff * vec[c] * proj[...]).astype(BF16)

    def tree():
        chunks = r_buf.shape[0]
        near = edge_dev(me_e + 1 - 2 * (me_e % 2))
        across = edge_dev(3 - me_e)
        middle = (me_e == 1) | (me_e == 2)
        is_end = (me_e == 0) | (me_e == 3)

        def inward(k):
            return copy(part_buf.at[k], got_buf.at[k], rs_ss.at[k], rs_rs.at[k], near)

        def over(k):
            return copy(part_buf.at[k], y_buf.at[k], y_ss.at[k], y_rs.at[k], across)

        def outward(k):
            return copy(r_buf.at[k], r_buf.at[k], ag_ss.at[k], ag_rs.at[k], near)

        for k in range(0, chunks, 2):
            at = slice(k * 128, k * 128 + 256)
            m = dot(contrib[...], hot_s[at, :], NT) - refs[:, at]
            part_buf[k] = m[:, :128]
            part_buf[k + 1] = m[:, 128:]

            @pl.when(is_end)
            def _(k=k):
                inward(k).start()
                inward(k + 1).start()

        square = jnp.zeros((1, 1), F32)
        for k in range(chunks + 1):
            @pl.when(middle)
            def _(k=k):
                if k < chunks:
                    inward(k).wait_recv()
                    part_buf[k] += got_buf[k]
                    over(k).start()
                if k:
                    over(k - 1).wait_recv()
                    r_buf[k - 1] = part_buf[k - 1] + y_buf[k - 1]
                    outward(k - 1).start()

            if k:
                @pl.when(is_end)
                def _(k=k):
                    outward(k - 1).wait_recv()

            if k and k % 2 == 0:
                r = jnp.concatenate([r_buf[k - 2], r_buf[k - 1]], axis=1)
                hi, lo = split(r, 2)
                both = jnp.concatenate([hi, lo], axis=0)
                for i in range(edges // lanes):
                    cut = slice(i * lanes, (i + 1) * lanes)
                    x = dot(both, hot_s[(k - 2) * 128:k * 128, cut])
                    rd[:, cut] += x[:3 * share] + x[3 * share:]
                square = square + jnp.sum(jnp.sum(r * r, axis=0, keepdims=True), axis=1, keepdims=True)

        @pl.when(is_end)
        def _():
            for k in range(chunks):
                inward(k).wait_send()

        @pl.when(middle)
        def _():
            for k in range(chunks):
                over(k).wait_send()
                outward(k).wait_send()

        return square

    def direct():
        def model(q):
            at = pl.ds(pl.multiple_of(q * piece, piece), piece)
            return dot(contrib[...], hot_s[at, :], NT) - refs[:, at]

        def rs_copy(i, q, src):
            return copy(part_buf.at[q], got_buf.at[src], rs_ss.at[i], rs_rs.at[src], edge_dev(q))

        def send_piece(i):
            q = (me_e + i + 1) % n_e

            def go():
                part_buf[q] = model(q)
                rs_copy(i, q, me_e).start()

            if own_n == n_e:
                go()
            else:
                pl.when(q < own_n)(go)

        loop(n_e - 1, send_piece)

        def own():
            got_buf[me_e] = model(me_e)

            def wait(i):
                j = (me_e + i + 1) % n_e
                copy(got_buf.at[j], got_buf.at[j], rs_ss.at[i], rs_rs.at[j], edge_dev(j)).wait_recv()

            loop(n_e - 1, wait)
            r_buf[me_e] = total(got_buf, n_e)

            def give(i):
                q = (me_e + i + 1) % n_e
                copy(r_buf.at[me_e], r_buf.at[me_e], ag_ss.at[i], ag_rs.at[me_e], edge_dev(q)).start()

            loop(n_e - 1, give)

        if own_n == n_e:
            own()
        else:
            pl.when(me_e < own_n)(own)

        def use(q, square):
            r = r_buf[q]
            hi, lo = split(r, 2)
            both = jnp.concatenate([hi, lo], axis=0)
            at = pl.ds(pl.multiple_of(q * piece, piece), piece)
            for i in range(edges // lanes):
                cut = slice(i * lanes, (i + 1) * lanes)
                x = dot(both, hot_s[at, cut])
                rd[:, cut] += x[:3 * share] + x[3 * share:]
            return square + jnp.sum(jnp.sum(r * r, axis=0, keepdims=True), axis=1, keepdims=True)

        square = jnp.zeros((1, 1), F32)
        for i in range(n_e):
            q = (me_e + i) % n_e
            if i:
                def wait(q=q):
                    copy(r_buf.at[q], r_buf.at[q], ag_ss.at[0], ag_rs.at[q], edge_dev(q)).wait_recv()
                if own_n == n_e:
                    wait()
                else:
                    pl.when(q < own_n)(wait)
            if own_n == n_e:
                square = use(q, square)
        if own_n != n_e:
            square = lax.fori_loop(0, own_n, use, square)
        def sent(i):
            q = (me_e + i + 1) % n_e

            def go():
                rs_copy(i, q, me_e).wait_send()

            if own_n == n_e:
                go()
            else:
                pl.when(q < own_n)(go)

        loop(n_e - 1, sent)

        def ag_sent():
            loop(n_e - 1, lambda i: copy(
                r_buf.at[me_e], r_buf.at[me_e], ag_ss.at[i], ag_rs.at[me_e], edge_dev((me_e + i + 1) % n_e)).wait_send())

        if own_n == n_e:
            ag_sent()
        else:
            pl.when(me_e < own_n)(ag_sent)
        return square

    rd[...] = jnp.zeros_like(rd)
    if n_e == 4:
        square = tree()
    else:
        square = direct()

    rproj = vec[0] * rd[:share]
    for c in (1, 2):
        rproj = rproj + vec[c] * rd[c * share:(c + 1) * share]
    dst = (2.0 / probes_total) * jnp.sum(proj[...] * rproj, axis=0, keepdims=True)
    dz_part = dst * sig_z
    n_w = n_e * n_p
    me_w = me_e * n_p + me_p
    w_dev = lambda f: dev(f // n_p, me_r, f % n_p)
    p_dev = lambda p: dev(me_e, me_r, p)
    w_buf[me_w, :, :atoms] = row_dot(dz_part, hot_r[...], NT)
    w_buf[me_w, :, atoms:] = jnp.broadcast_to(square, (1, 128))
    z_buf[me_p] = dz_part
    spread(w_buf, w_ss, w_rs, me_w, n_w, w_dev)
    spread(z_buf, z_ss, z_rs, me_p, n_p, p_dev)

    for q in range(own_n):
        for c in range(3):
            x = r_buf[q, c * share:(c + 1) * share, :]
            res_out[pl.ds(q * piece * 3 + c, piece, stride=3), :] = x.T

    gathered(w_buf, w_ss, w_rs, me_w, n_w, w_dev)
    gathered(z_buf, z_ss, z_rs, me_p, n_p, p_dev)
    weight = total(w_buf, n_w)[:, :atoms]
    squares = w_buf[me_e * n_p, :, atoms:]
    for p in range(1, n_p):
        squares = squares + w_buf[me_e * n_p + p, :, atoms:]
    mse_out[...] = squares / (3 * atoms * probes_total)
    dz = total(z_buf, n_p)
    wr = row_dot(weight, hot_r[...])

    dz_hi, dz_lo = split(dz, 2)
    wr_hi, wr_lo = split(wr, 2)
    sums = dot(stack_rows([dz_hi, dz_lo, wr_hi, wr_lo]), latent[...])
    g_members = n_e * n_r
    me_g = me_e * n_r + me_r
    g_dev = lambda f: dev(f // n_r, f % n_r, me_p)
    v_buf[me_g] = jnp.zeros(v_buf.shape[1:], F32)
    v_buf[me_g, 0:1] = sums[0:1] + sums[1:2]
    v_buf[me_g, 1:2] = sums[2:3] + sums[3:4]
    spread(v_buf, v_ss, v_rs, me_g, g_members, g_dev)

    ws = w_stiff[...].astype(F32)
    ws_half = ws[:, :half]
    u_half = u[:, :half]
    for p in range(1, n_p):
        ws_half = jnp.where(me_p == p, ws[:, p * half:(p + 1) * half], ws_half)
        u_half = jnp.where(me_p == p, u[:, p * half:(p + 1) * half], u_half)
    uh_hi, uh_lo = split(u_half, 2)
    dlat = dot(
        stack_rows([dz_hi, dz_lo, wr_hi, wr_hi, wr_lo]),
        stack_rows([ws_half, ws_half, uh_hi, uh_lo, uh_hi]), TN)
    x = pre[me_p]
    sg = sigmoid(x)
    dpre = (dlat * sg * (1.0 + x * (1.0 - sg))).astype(BF16)
    g_half = dot(feats[0], dpre, TN)
    g_own, g_rows = gf_buf.shape[1], gf_buf.shape[2]
    g_buf[...] = g_half.reshape(g_buf.shape)

    def g_send(i):
        q = (me_g + i + 1) % g_members

        def go():
            copy(g_buf.at[q], gg_buf.at[me_g], g_ss.at[i], g_rs.at[me_g], g_dev(q)).start()

        if g_own == g_members:
            go()
        else:
            pl.when(q < g_own)(go)

    loop(g_members - 1, g_send)

    def gf_copy(i, g, p, f):
        return copy(gf_buf.at[p, g], gf_buf.at[p, g], gf_ss.at[i], gf_rs.at[p, g], all_dev(f))

    def g_own_part():
        gg_buf[me_g] = g_buf[me_g]

        def wait(i):
            j = (me_g + i + 1) % g_members
            copy(gg_buf.at[j], gg_buf.at[j], g_ss.at[i], g_rs.at[j], g_dev(j)).wait_recv()

        loop(g_members - 1, wait)
        gf_buf[me_p, me_g] = total(gg_buf, g_members)

        def give(i):
            gf_copy(i, me_g, me_p, (me_all + i + 1) % n_all).start()

        loop(n_all - 1, give)

    if g_own == g_members:
        g_own_part()
    else:
        pl.when(me_g < g_own)(g_own_part)

    gathered(v_buf, v_ss, v_rs, me_g, g_members, g_dev)
    v = total(v_buf, g_members)
    gstiff_out[...] = v[0:1]
    q_row = v[1:2]
    q_hi, q_lo = split(q_row, 2)
    e_hi, e_lo = split(wenv, 2)
    gmsg_out[...] = dot(stack_rows([q_hi, q_hi, q_lo]), stack_rows([e_hi, e_lo, e_hi]), TN)
    genv_out[...] = row_dot(q_row, w_msg[...])

    def g_arrive(i):
        f = (me_all + i + 1) % n_all
        p, g = f % n_p, f // n_p

        def go():
            gf_copy(i, g, p, f).wait_recv()

        if g_own == g_members:
            go()
        else:
            pl.when(g < g_own)(go)

    loop(n_all - 1, g_arrive)
    for p in range(n_p):
        gin_out[:, p * half:(p + 1) * half] = gf_buf[p].reshape(width, half)

    def g_sent(i):
        q = (me_g + i + 1) % g_members

        def go():
            copy(g_buf.at[q], gg_buf.at[me_g], g_ss.at[i], g_rs.at[me_g], g_dev(q)).wait_send()

        if g_own == g_members:
            go()
        else:
            pl.when(q < g_own)(go)

    loop(g_members - 1, g_sent)

    def gf_sent():
        loop(n_all - 1, lambda i: gf_copy(i, me_g, me_p, (me_all + i + 1) % n_all).wait_send())

    if g_own == g_members:
        gf_sent()
    else:
        pl.when(me_g < g_own)(gf_sent)


def body(
    n_e, n_r, n_p,
    edge_feats, edge_vecs, senders, receivers, tiles, tile_rows, tile_cols, tile_count,
    probes, w_in, w_msg, w_stiff, w_env,
):
    share = probes.shape[1]
    dim = probes.shape[0]
    atoms = dim // 3
    edges = senders.shape[1]
    width = w_in.shape[1]
    msg = w_msg.shape[1]
    vm = pl.BlockSpec(memory_space=pltpu.VMEM)
    sm = pl.BlockSpec(memory_space=pltpu.SMEM)
    pt, refs = pl.pallas_call(
        tile_kernel,
        out_shape=(
            jax.ShapeDtypeStruct((3 * share, atoms), BF16),
            jax.ShapeDtypeStruct((3 * share, atoms), F32),
        ),
        in_specs=[sm, sm, sm, vm, vm],
        out_specs=(vm, vm),
        scratch_shapes=[
            pltpu.VMEM((dim // TILE, TILE, share), BF16),
            pltpu.VMEM((dim, 128), F32),
            pltpu.VMEM((dim, 128), F32),
        ],
        compiler_params=pltpu.CompilerParams(vmem_limit_bytes=40 * 2**20),
        name="tiles",
    )(tile_rows, tile_cols, tile_count, tiles, probes)

    own_n = atoms // 128 if n_e == 4 else min(n_e, atoms // 128)
    got_n = max(own_n, n_e)
    piece = atoms // own_n
    g_members = n_e * n_r
    g_own = min(g_members, width // 8)
    g_rows = width // g_own
    half = width // n_p
    n_all = n_e * n_r * n_p
    n_w = n_e * n_p
    sem = lambda *shape: pltpu.SemaphoreType.DMA(shape)
    vmem = pltpu.VMEM
    outs = pl.pallas_call(
        functools.partial(main_kernel, n_e, n_r, n_p, share * n_p),
        out_shape=(
            jax.ShapeDtypeStruct((dim, share), F32),
            jax.ShapeDtypeStruct((1, 128), F32),
            jax.ShapeDtypeStruct((width, width), F32),
            jax.ShapeDtypeStruct((width, msg), F32),
            jax.ShapeDtypeStruct((1, width), F32),
            jax.ShapeDtypeStruct((1, msg), F32),
        ),
        in_specs=[vm] * 10,
        out_specs=(vm,) * 6,
        scratch_shapes=[
            vmem((atoms, edges), BF16),
            vmem((atoms, edges), BF16),
            vmem((n_p, edges, half), F32),
            vmem((edges, width), BF16),
            vmem((share, edges), F32),
            vmem((3 * share, edges), BF16),
            vmem((3 * share, edges), F32),
            vmem((n_e, 1, atoms), F32),
            vmem((own_n, 3 * share, piece), F32),
            vmem((got_n, 3 * share, piece), F32),
            vmem((own_n, 3 * share, piece), F32),
            vmem((own_n, 3 * share, piece), F32),
            vmem((n_w, 1, atoms + 128), F32),
            vmem((n_p, 1, edges), F32),
            vmem((g_own, g_rows, half), F32),
            vmem((g_members, g_rows, half), F32),
            vmem((n_p, g_own, g_rows, half), F32),
            vmem((g_members, 8, width), F32),
            sem(n_e), sem(n_e),
            sem(got_n), sem(got_n),
            sem(got_n), sem(got_n),
            sem(got_n), sem(got_n),
            sem(n_w), sem(n_w),
            sem(n_p), sem(n_p),
            sem(g_members), sem(g_members),
            sem(n_all), sem(n_p, g_members),
            sem(g_members), sem(g_members),
        ],
        compiler_params=pltpu.CompilerParams(
            collective_id=0, has_side_effects=True, vmem_limit_bytes=48 * 2**20),
        name="edges",
    )(
        edge_feats, edge_vecs, senders, receivers, pt, refs, w_in, w_msg,
        w_stiff.reshape(1, -1), w_env.reshape(1, -1),
    )
    residual, mse, g_in, g_msg, g_stiff, g_env = outs
    return (residual[None], mse[0, :1], g_in, g_msg, g_stiff[0], g_env[0])


def solution(mesh):
    n_e, n_r, n_p = mesh.shape["edge"], mesh.shape["replica"], mesh.shape["probe"]
    return jax.shard_map(
        functools.partial(body, n_e, n_r, n_p),
        mesh=mesh,
        in_specs=(
            P(("groups", "replica"), "edge", None),
            P(("groups", "replica"), None, "edge"),
            P(("groups", "replica"), "edge"),
            P(("groups", "replica"), "edge"),
            P(("groups", "replica"), "edge", None, None),
            P(("groups", "replica"), "edge"),
            P(("groups", "replica"), "edge"),
            P(("groups", "replica"), "edge"),
            P(None, "probe"),
            P(),
            P(),
            P(),
            P(),
        ),
        out_specs=(
            P(("groups", "replica"), None, "probe"),
            P(("groups", "replica")),
            P("groups", None),
            P("groups", None),
            P("groups"),
            P("groups"),
        ),
        check_vma=False,
    )
```

```python
import functools

import jax
import jax.numpy as jnp
from jax import lax
from jax.experimental import pallas as pl
from jax.experimental.pallas import tpu as pltpu
from jax.sharding import PartitionSpec as P

TILE = 128
MESH = pl.DeviceIdType.MESH
F32 = jnp.float32
BF16 = jnp.bfloat16
NN = (((1,), (0,)), ((), ()))
NT = (((1,), (1,)), ((), ()))
TN = (((0,), (0,)), ((), ()))


def dot(a, b, dims=NN):
    return lax.dot_general(a, b, dims, preferred_element_type=F32)


def split(x, parts):
    out = []
    for _ in range(parts):
        piece = x.astype(BF16)
        out.append(piece)
        x = x - piece.astype(F32)
    return out


def stack_rows(rows):
    n = rows[0].shape[1]
    where = lax.broadcasted_iota(jnp.int32, (8, n), 0)
    out = jnp.zeros((8, n), F32)
    for i, row in enumerate(rows):
        out = jnp.where(where == i, row.astype(F32), out)
    return out.astype(BF16)


def row_dot(x, b, dims=NN, parts=3):
    return jnp.sum(dot(stack_rows(split(x, parts)), b, dims), axis=0, keepdims=True)


def sigmoid(x):
    return 1.0 / (1.0 + jnp.exp(-x))


def loop(count, fn):
    if count <= 16:
        for i in range(count):
            fn(i)
    else:
        def step(i, carry):
            fn(i)
            return carry
        lax.fori_loop(0, count, step, 0)


def tile_kernel(rows, cols, count, tiles, probes, pt_ref, ref_ref, pb, pf, acc):
    n_slots = tiles.shape[1]
    atoms = pt_ref.shape[1]
    share = probes.shape[0]
    pv = probes[...].astype(F32).T
    pf[:, :share] = pv
    pb[...] = pv.astype(BF16).reshape(pb.shape)
    acc[...] = jnp.zeros_like(acc)
    live = count[0, 0]
    unroll = 8 if n_slots % 8 == 0 else 1

    def step(i, carry):
        for j in range(unroll):
            t = i * unroll + j
            prod = dot(tiles[0, t], pb[cols[0, t]])
            prod = jnp.where(t < live, prod, 0.0)
            at = pl.ds(pl.multiple_of(rows[0, t] * TILE, TILE), TILE)
            acc[at, :share] += prod
        return carry

    lax.fori_loop(0, (live + unroll - 1) // unroll, step, 0)
    for c in range(3):
        pick = pl.ds(c, atoms, stride=3)
        pt_ref[c * share:(c + 1) * share, :] = pf[pick, :].T[:share].astype(BF16)
        ref_ref[c * share:(c + 1) * share, :] = acc[pick, :].T[:share]


def main_kernel(
    n_e, n_r, n_p, probes_total,
    feats, vecs, send, recv, pt, refs, w_in, w_msg, w_stiff, w_env,
    res_out, mse_out, gin_out, gmsg_out, gstiff_out, genv_out,
    hot_r, hot_s, pre, latent, proj, contrib, rd, res_s, feats_t,
    s_buf, part_buf, got_buf, y_buf, r_buf, w_buf, z_buf, g_buf, gg_buf, gf_buf, v_buf,
    s_ss, s_rs, rs_ss, rs_rs, y_ss, y_rs, ag_ss, ag_rs, w_ss, w_rs, z_ss, z_rs, g_ss, g_rs, gf_ss, gf_rs, fw_ss, v_ss, v_rs,
):
    edges = send.shape[1]
    atoms = pt.shape[1]
    share = pt.shape[0] // 3
    width = w_in.shape[1]
    half = width // n_p
    own_n, piece = r_buf.shape[0], r_buf.shape[2]
    lanes = 256
    me_e, me_r, me_p = lax.axis_index("edge"), lax.axis_index("replica"), lax.axis_index("probe")

    def dev(e, r, p):
        return {"edge": e, "replica": r, "probe": p}

    def copy(src, dst, ss, rs, device):
        return pltpu.make_async_remote_copy(
            src_ref=src, dst_ref=dst, send_sem=ss, recv_sem=rs, device_id=device, device_id_type=MESH)

    barrier = pltpu.get_barrier_semaphore()
    n_all = n_e * n_r * n_p
    me_all = (me_e * n_r + me_r) * n_p + me_p

    def all_dev(f):
        return dev(f // (n_r * n_p), (f // n_p) % n_r, f % n_p)

    def greet(i):
        pl.semaphore_signal(barrier, inc=1, device_id=all_dev((me_all + i + 1) % n_all), device_id_type=MESH)

    loop(n_all - 1, greet)

    def spread(buf, ss, rs, me, n, device):
        def go(i):
            copy(buf.at[me], buf.at[me], ss.at[i], rs.at[me], device((me + i + 1) % n)).start()
        loop(n - 1, go)

    def gathered(buf, ss, rs, me, n, device):
        def go(i):
            j = (me + i + 1) % n
            c = copy(buf.at[j], buf.at[j], ss.at[i], rs.at[j], device(j))
            c.wait_recv()
            c.wait_send()
        loop(n - 1, go)

    def total(buf, n):
        if n <= 16:
            out = buf[0]
            for j in range(1, n):
                out = out + buf[j]
            return out
        return lax.fori_loop(1, n, lambda j, t: t + buf[j], buf[0])

    wenv = w_env[...]
    u = row_dot(wenv, w_msg[...], NT)
    u_hi, u_lo = split(u, 2)
    ws = w_stiff[...].astype(F32).reshape(1, -1)
    readout = stack_rows([ws, u_hi, u_lo])
    rows = 256 if edges % 256 == 0 else edges

    def forward(i, carry):
        at = pl.ds(pl.multiple_of(i * rows, rows), rows)
        x = dot(feats[0, at, :], w_in[...])
        for p in range(n_p):
            pre[p, at, :] = x[:, p * half:(p + 1) * half]
        latent[at, :] = (x * sigmoid(x)).astype(BF16)
        return carry

    lax.fori_loop(0, edges // rows, forward, 0)

    snd, rcv = send[...], recv[...]

    def hots(i, carry):
        base = i * 32
        ids = lax.broadcasted_iota(jnp.int32, (32, edges), 0) + base
        at = pl.ds(pl.multiple_of(base, 32), 32)
        hot_r[at, :] = jnp.where(ids == rcv, 1.0, 0.0).astype(BF16)
        return carry

    def signed_hots(i, carry):
        base = i * 32
        ids = lax.broadcasted_iota(jnp.int32, (32, edges), 0) + base
        at = pl.ds(pl.multiple_of(base, 32), 32)
        r = jnp.where(ids == rcv, 1.0, 0.0)
        s = jnp.where(ids == snd, 1.0, 0.0)
        hot_s[at, :] = (s - r).astype(BF16)
        return carry

    lax.fori_loop(0, atoms // 32, hots, 0)
    read = dot(readout, latent[...], NT)
    lw = read[0:1]
    mw = read[1:2] + read[2:3]
    s_buf[me_e] = row_dot(mw, hot_r[...], NT)
    pl.semaphore_wait(barrier, n_all - 1)
    edge_dev = lambda e: dev(e, me_r, me_p)
    spread(s_buf, s_ss, s_rs, me_e, n_e, edge_dev)

    vec = [vecs[c] for c in range(3)]

    def project(i, carry):
        at = pl.ds(pl.multiple_of(i * lanes, lanes), lanes)
        delta = dot(pt[...], hot_s[:, at])
        out = vecs[0, :, at] * delta[:share]
        for c in (1, 2):
            out = out + vecs[c, :, at] * delta[c * share:(c + 1) * share]
        proj[:, at] = out
        return carry

    lax.fori_loop(0, atoms // 32, signed_hots, 0)
    lax.fori_loop(0, edges // lanes, project, 0)
    gathered(s_buf, s_ss, s_rs, me_e, n_e, edge_dev)
    zeta = lw + row_dot(total(s_buf, n_e), hot_r[...])
    stiff = jnp.maximum(zeta, 0.0) + jnp.log1p(jnp.exp(-jnp.abs(zeta)))
    sig_z = sigmoid(zeta)
    for c in range(3):
        contrib[c * share:(c + 1) * share, :] = (stiff * vec[c] * proj[...]).astype(BF16)

    def slope():
        x = pre[me_p]
        sg = sigmoid(x)
        pre[me_p] = sg * (1.0 + x * (1.0 - sg))

    def turn():
        feats_t[...] = feats[0].T

    def tree():
        chunks = r_buf.shape[0]
        near = edge_dev(me_e + 1 - 2 * (me_e % 2))
        across = edge_dev(3 - me_e)
        middle = (me_e == 1) | (me_e == 2)
        is_end = (me_e == 0) | (me_e == 3)

        def inward(k):
            return copy(part_buf.at[k], got_buf.at[k], rs_ss.at[k], rs_rs.at[k], near)

        def over(k):
            return copy(part_buf.at[k], y_buf.at[k], y_ss.at[k], y_rs.at[k], across)

        def outward(k):
            return copy(r_buf.at[k], r_buf.at[k], ag_ss.at[k], ag_rs.at[k], near)

        for k in range(0, chunks, 2):
            at = slice(k * 128, k * 128 + 256)
            m = dot(contrib[...], hot_s[at, :], NT) - refs[:, at]
            part_buf[k] = m[:, :128]
            part_buf[k + 1] = m[:, 128:]

            @pl.when(is_end)
            def _(k=k):
                inward(k).start()
                inward(k + 1).start()

        square = jnp.zeros((1, 1), F32)
        for k in range(chunks + 1):
            @pl.when(middle)
            def _(k=k):
                if k < chunks:
                    inward(k).wait_recv()
                    part_buf[k] += got_buf[k]
                    over(k).start()
                if k:
                    over(k - 1).wait_recv()
                    r_buf[k - 1] = part_buf[k - 1] + y_buf[k - 1]
                    outward(k - 1).start()

            if k == 1:
                slope()
            if k == 3:
                turn()
            if k:
                @pl.when(is_end)
                def _(k=k):
                    outward(k - 1).wait_recv()

            if k and k % 2 == 0:
                r = jnp.concatenate([r_buf[k - 2], r_buf[k - 1]], axis=1)
                hi, lo = split(r, 2)
                both = jnp.concatenate([hi, lo], axis=0)
                for i in range(edges // lanes):
                    cut = slice(i * lanes, (i + 1) * lanes)
                    x = dot(both, hot_s[(k - 2) * 128:k * 128, cut])
                    rd[:, cut] += x[:3 * share] + x[3 * share:]
                square = square + jnp.sum(jnp.sum(r * r, axis=0, keepdims=True), axis=1, keepdims=True)

        @pl.when(is_end)
        def _():
            for k in range(chunks):
                inward(k).wait_send()

        @pl.when(middle)
        def _():
            for k in range(chunks):
                over(k).wait_send()
                outward(k).wait_send()

        return square

    def direct():
        def model(q):
            at = pl.ds(pl.multiple_of(q * piece, piece), piece)
            return dot(contrib[...], hot_s[at, :], NT) - refs[:, at]

        def rs_copy(i, q, src):
            return copy(part_buf.at[q], got_buf.at[src], rs_ss.at[i], rs_rs.at[src], edge_dev(q))

        def send_piece(i):
            q = (me_e + i + 1) % n_e

            def go():
                part_buf[q] = model(q)
                rs_copy(i, q, me_e).start()

            if own_n == n_e:
                go()
            else:
                pl.when(q < own_n)(go)

        loop(n_e - 1, send_piece)

        def own():
            got_buf[me_e] = model(me_e)

            def wait(i):
                j = (me_e + i + 1) % n_e
                copy(got_buf.at[j], got_buf.at[j], rs_ss.at[i], rs_rs.at[j], edge_dev(j)).wait_recv()

            loop(n_e - 1, wait)
            r_buf[me_e] = total(got_buf, n_e)

            def give(i):
                q = (me_e + i + 1) % n_e
                copy(r_buf.at[me_e], r_buf.at[me_e], ag_ss.at[i], ag_rs.at[me_e], edge_dev(q)).start()

            loop(n_e - 1, give)

        if own_n == n_e:
            own()
        else:
            pl.when(me_e < own_n)(own)

        def use(q, square):
            r = r_buf[q]
            hi, lo = split(r, 2)
            both = jnp.concatenate([hi, lo], axis=0)
            at = pl.ds(pl.multiple_of(q * piece, piece), piece)
            for i in range(edges // lanes):
                cut = slice(i * lanes, (i + 1) * lanes)
                x = dot(both, hot_s[at, cut])
                rd[:, cut] += x[:3 * share] + x[3 * share:]
            return square + jnp.sum(jnp.sum(r * r, axis=0, keepdims=True), axis=1, keepdims=True)

        square = jnp.zeros((1, 1), F32)
        for i in range(n_e):
            q = (me_e + i) % n_e
            if i:
                def wait(q=q):
                    copy(r_buf.at[q], r_buf.at[q], ag_ss.at[0], ag_rs.at[q], edge_dev(q)).wait_recv()
                if own_n == n_e:
                    wait()
                else:
                    pl.when(q < own_n)(wait)
            if own_n == n_e:
                square = use(q, square)
        if own_n != n_e:
            square = lax.fori_loop(0, own_n, use, square)
        def sent(i):
            q = (me_e + i + 1) % n_e

            def go():
                rs_copy(i, q, me_e).wait_send()

            if own_n == n_e:
                go()
            else:
                pl.when(q < own_n)(go)

        loop(n_e - 1, sent)

        def ag_sent():
            loop(n_e - 1, lambda i: copy(
                r_buf.at[me_e], r_buf.at[me_e], ag_ss.at[i], ag_rs.at[me_e], edge_dev((me_e + i + 1) % n_e)).wait_send())

        if own_n == n_e:
            ag_sent()
        else:
            pl.when(me_e < own_n)(ag_sent)
        return square

    rd[...] = jnp.zeros_like(rd)
    if n_e == 4:
        square = tree()
    else:
        square = direct()
        slope()
        turn()

    rproj = vec[0] * rd[:share]
    for c in (1, 2):
        rproj = rproj + vec[c] * rd[c * share:(c + 1) * share]
    dst = (2.0 / probes_total) * jnp.sum(proj[...] * rproj, axis=0, keepdims=True)
    dz_part = dst * sig_z
    n_w = n_e * n_p
    me_w = me_e * n_p + me_p
    w_dev = lambda f: dev(f // n_p, me_r, f % n_p)
    p_dev = lambda p: dev(me_e, me_r, p)
    w_buf[me_w, :, :atoms] = row_dot(dz_part, hot_r[...], NT)
    w_buf[me_w, :, atoms:] = jnp.broadcast_to(square, (1, 128))
    z_buf[me_p] = dz_part
    spread(w_buf, w_ss, w_rs, me_w, n_w, w_dev)
    spread(z_buf, z_ss, z_rs, me_p, n_p, p_dev)

    for q in range(own_n):
        for c in range(3):
            x = r_buf[q, c * share:(c + 1) * share, :]
            res_s[pl.ds(q * piece * 3 + c, piece, stride=3), :] = x.T
    for b in range(3 * atoms // 128):
        res_out[:, b * 128:(b + 1) * 128] = res_s[b * 128:(b + 1) * 128, :].T

    gathered(w_buf, w_ss, w_rs, me_w, n_w, w_dev)
    gathered(z_buf, z_ss, z_rs, me_p, n_p, p_dev)
    weight = total(w_buf, n_w)[:, :atoms]
    squares = w_buf[me_e * n_p, :, atoms:]
    for p in range(1, n_p):
        squares = squares + w_buf[me_e * n_p + p, :, atoms:]
    mse_out[...] = squares / (3 * atoms * probes_total)
    dz = total(z_buf, n_p)
    wr = row_dot(weight, hot_r[...])

    dz_hi, dz_lo = split(dz, 2)
    wr_hi, wr_lo = split(wr, 2)
    sums = dot(stack_rows([dz_hi, dz_lo, wr_hi, wr_lo]), latent[...])
    g_members = n_e * n_r
    me_g = me_e * n_r + me_r
    g_dev = lambda f: dev(f // n_r, f % n_r, me_p)
    v_buf[me_g, 0:1] = sums[0:1] + sums[1:2]
    v_buf[me_g, 1:2] = sums[2:3] + sums[3:4]
    spread(v_buf, v_ss, v_rs, me_g, g_members, g_dev)

    ws_half = ws[:, :half]
    u_half = u[:, :half]
    for p in range(1, n_p):
        ws_half = jnp.where(me_p == p, ws[:, p * half:(p + 1) * half], ws_half)
        u_half = jnp.where(me_p == p, u[:, p * half:(p + 1) * half], u_half)
    uh_hi, uh_lo = split(u_half, 2)
    dlat = dot(
        stack_rows([dz_hi, dz_lo, wr_hi, wr_hi, wr_lo]),
        stack_rows([ws_half, ws_half, uh_hi, uh_lo, uh_hi]), TN)
    dpre = (dlat * pre[me_p]).astype(BF16)
    g_half = dot(feats_t[...], dpre)
    g_own, g_rows = gf_buf.shape[1], gf_buf.shape[2]
    g_buf[...] = g_half.reshape(g_buf.shape)

    def g_send(i):
        q = (me_g + i + 1) % g_members

        def go():
            copy(g_buf.at[q], gg_buf.at[me_g], g_ss.at[i], g_rs.at[me_g], g_dev(q)).start()

        if g_own == g_members:
            go()
        else:
            pl.when(q < g_own)(go)

    loop(g_members - 1, g_send)

    def gf_copy(i, g, f):
        return copy(gf_buf.at[me_p, g], gf_buf.at[me_p, g], gf_ss.at[i], gf_rs.at[me_p, g], g_dev(f))

    def forward_copy(o, g):
        return copy(
            gf_buf.at[me_p, g], gf_buf.at[me_p, g], fw_ss.at[o - 1, g], gf_rs.at[me_p, g],
            p_dev((me_p + o) % n_p))

    def when_owned(g, fn):
        if g_own == g_members:
            fn()
        else:
            pl.when(g < g_own)(fn)

    def g_own_part():
        gg_buf[me_g] = g_buf[me_g]

        def wait(i):
            j = (me_g + i + 1) % g_members
            copy(gg_buf.at[j], gg_buf.at[j], g_ss.at[i], g_rs.at[j], g_dev(j)).wait_recv()

        loop(g_members - 1, wait)
        gf_buf[me_p, me_g] = total(gg_buf, g_members)

        loop(g_members - 1, lambda i: gf_copy(i, me_g, (me_g + i + 1) % g_members).start())
        for o in range(1, n_p):
            forward_copy(o, me_g).start()

    if g_own == g_members:
        g_own_part()
    else:
        pl.when(me_g < g_own)(g_own_part)

    gathered(v_buf, v_ss, v_rs, me_g, g_members, g_dev)
    v = total(v_buf, g_members)
    gstiff_out[...] = v[0:1]
    q_row = v[1:2]
    q_hi, q_lo = split(q_row, 2)
    e_hi, e_lo = split(wenv, 2)
    gmsg_out[...] = dot(stack_rows([q_hi, q_hi, q_lo]), stack_rows([e_hi, e_lo, e_hi]), TN)
    genv_out[...] = row_dot(q_row, w_msg[...])

    def pass_on(i):
        g = (me_g + i + 1) % g_members

        def go():
            gf_copy(i, g, g).wait_recv()
            for o in range(1, n_p):
                forward_copy(o, g).start()

        when_owned(g, go)

    loop(g_members - 1, pass_on)

    def from_partner(i):
        g = (me_g + i) % g_members

        def go():
            for o in range(1, n_p):
                p = (me_p + o) % n_p
                copy(gf_buf.at[p, g], gf_buf.at[p, g], fw_ss.at[o - 1, g], gf_rs.at[p, g], p_dev(p)).wait_recv()

        when_owned(g, go)

    loop(g_members, from_partner)
    for p in range(n_p):
        gin_out[:, p * half:(p + 1) * half] = gf_buf[p].reshape(width, half)

    def g_sent(i):
        q = (me_g + i + 1) % g_members

        def go():
            copy(g_buf.at[q], gg_buf.at[me_g], g_ss.at[i], g_rs.at[me_g], g_dev(q)).wait_send()

        if g_own == g_members:
            go()
        else:
            pl.when(q < g_own)(go)

    loop(g_members - 1, g_sent)

    when_owned(me_g, lambda: loop(
        g_members - 1, lambda i: gf_copy(i, me_g, (me_g + i + 1) % g_members).wait_send()))

    def passed(i):
        def go():
            for o in range(1, n_p):
                forward_copy(o, i).wait_send()

        when_owned(i, go)

    loop(g_members, passed)


def body(
    n_e, n_r, n_p,
    edge_feats, edge_vecs, senders, receivers, tiles, tile_rows, tile_cols, tile_count,
    probes, w_in, w_msg, w_stiff, w_env,
):
    share = probes.shape[1]
    dim = probes.shape[0]
    atoms = dim // 3
    edges = senders.shape[1]
    width = w_in.shape[1]
    msg = w_msg.shape[1]
    vm = pl.BlockSpec(memory_space=pltpu.VMEM)
    sm = pl.BlockSpec(memory_space=pltpu.SMEM)
    pt, refs = pl.pallas_call(
        tile_kernel,
        out_shape=(
            jax.ShapeDtypeStruct((3 * share, atoms), BF16),
            jax.ShapeDtypeStruct((3 * share, atoms), F32),
        ),
        in_specs=[sm, sm, sm, vm, vm],
        out_specs=(vm, vm),
        scratch_shapes=[
            pltpu.VMEM((dim // TILE, TILE, share), BF16),
            pltpu.VMEM((dim, 128), F32),
            pltpu.VMEM((dim, 128), F32),
        ],
        compiler_params=pltpu.CompilerParams(vmem_limit_bytes=40 * 2**20),
        name="tiles",
    )(tile_rows, tile_cols, tile_count, tiles, probes.T)

    own_n = atoms // 128 if n_e == 4 else min(n_e, atoms // 128)
    got_n = max(own_n, n_e)
    piece = atoms // own_n
    g_members = n_e * n_r
    g_own = min(g_members, width // 8)
    g_rows = width // g_own
    half = width // n_p
    n_w = n_e * n_p
    sem = lambda *shape: pltpu.SemaphoreType.DMA(shape)
    vmem = pltpu.VMEM
    outs = pl.pallas_call(
        functools.partial(main_kernel, n_e, n_r, n_p, share * n_p),
        out_shape=(
            jax.ShapeDtypeStruct((share, dim), F32),
            jax.ShapeDtypeStruct((1, 128), F32),
            jax.ShapeDtypeStruct((width, width), F32),
            jax.ShapeDtypeStruct((width, msg), F32),
            jax.ShapeDtypeStruct((1, width), F32),
            jax.ShapeDtypeStruct((1, msg), F32),
        ),
        in_specs=[vm] * 10,
        out_specs=(vm,) * 6,
        scratch_shapes=[
            vmem((atoms, edges), BF16),
            vmem((atoms, edges), BF16),
            vmem((n_p, edges, half), F32),
            vmem((edges, width), BF16),
            vmem((share, edges), F32),
            vmem((3 * share, edges), BF16),
            vmem((3 * share, edges), F32),
            vmem((dim, share), F32),
            vmem((width, edges), BF16),
            vmem((n_e, 1, atoms), F32),
            vmem((own_n, 3 * share, piece), F32),
            vmem((got_n, 3 * share, piece), F32),
            vmem((own_n, 3 * share, piece), F32),
            vmem((own_n, 3 * share, piece), F32),
            vmem((n_w, 1, atoms + 128), F32),
            vmem((n_p, 1, edges), F32),
            vmem((g_own, g_rows, half), F32),
            vmem((g_members, g_rows, half), F32),
            vmem((n_p, g_own, g_rows, half), F32),
            vmem((g_members, 2, width), F32),
            sem(n_e), sem(n_e),
            sem(got_n), sem(got_n),
            sem(got_n), sem(got_n),
            sem(got_n), sem(got_n),
            sem(n_w), sem(n_w),
            sem(n_p), sem(n_p),
            sem(g_members), sem(g_members),
            sem(g_members), sem(n_p, g_members), sem(max(n_p - 1, 1), g_members),
            sem(g_members), sem(g_members),
        ],
        compiler_params=pltpu.CompilerParams(
            collective_id=0, has_side_effects=True, vmem_limit_bytes=48 * 2**20),
        name="edges",
    )(
        edge_feats, edge_vecs.transpose(1, 0, 2), senders, receivers, pt, refs, w_in, w_msg,
        w_stiff, w_env.reshape(1, -1),
    )
    residual, mse, g_in, g_msg, g_stiff, g_env = outs
    return (residual.T[None], mse[0, :1], g_in, g_msg, g_stiff[0], g_env[0])


def solution(mesh):
    n_e, n_r, n_p = mesh.shape["edge"], mesh.shape["replica"], mesh.shape["probe"]
    return jax.shard_map(
        functools.partial(body, n_e, n_r, n_p),
        mesh=mesh,
        in_specs=(
            P(("groups", "replica"), "edge", None),
            P(("groups", "replica"), None, "edge"),
            P(("groups", "replica"), "edge"),
            P(("groups", "replica"), "edge"),
            P(("groups", "replica"), "edge", None, None),
            P(("groups", "replica"), "edge"),
            P(("groups", "replica"), "edge"),
            P(("groups", "replica"), "edge"),
            P(None, "probe"),
            P(),
            P(),
            P(),
            P(),
        ),
        out_specs=(
            P(("groups", "replica"), None, "probe"),
            P(("groups", "replica")),
            P("groups", None),
            P("groups", None),
            P("groups"),
            P("groups"),
        ),
        check_vma=False,
    )
```
